32 devices in a mesh: dp: 16 (over z, x, core), shard: 2 (over y).
Axes of the slice: x: 2, y: 2, z: 4, core: 2. Of those that a mesh axis runs over, the one named last changes fastest.
Arguments:
- tokens: bfloat16 [64, 1024, 960], P('dp', 'shard'), may hold values from -6 to 6
- positions: int32 [64, 1024], P('dp', 'shard'), may hold values from 0 to 1023, as said below
- attn_gain: bfloat16 [960], P('shard'), may hold values from 0.25 to 1.75
- w_query: bfloat16 [960, 960], P('shard'), may hold values from -0.375 to 0.375
- w_key: bfloat16 [960, 320], P('shard'), may hold values from -0.1875 to 0.1875
- w_value: bfloat16 [960, 320], P('shard'), may hold values from -0.1875 to 0.1875
- w_out: bfloat16 [960, 960], P('shard'), may hold values from -0.5 to 0.5
- mlp_gain: bfloat16 [960], P('shard'), may hold values from 0.25 to 1.75
- w_gate: bfloat16 [960, 2560], P('shard'), may hold values from -0.1875 to 0.1875
- w_up: bfloat16 [960, 2560], P('shard'), may hold values from -0.1875 to 0.1875
- w_down: bfloat16 [2560, 960], P('shard'), may hold values from -0.125 to 0.125
- cotangent: bfloat16 [64, 1024, 960], P('dp', 'shard'), may hold values from -6 to 6
Outputs:
- output: bfloat16 [64, 1024, 960], P('dp', 'shard')
- input_grad: float32 [64, 1024, 960], P('dp', 'shard')
- grad_attn_gain: float32 [960], P('shard')
- grad_query: float32 [960, 960], P('shard')
- grad_key: float32 [960, 320], P('shard')
- grad_value: float32 [960, 320], P('shard')
- grad_out: float32 [960, 960], P('shard')
- grad_mlp_gain: float32 [960], P('shard')
- grad_gate: float32 [960, 2560], P('shard')
- grad_up: float32 [960, 2560], P('shard')
- grad_down: float32 [2560, 960], P('shard')
The draws below stay inside these ranges and needn't reach their ends.
Inputs may be any that keep to these rules, and one draw needn't show every extreme that they name: `positions`: in each row the first entry is 0 and every later entry is 0 or one more than the entry before it. In each aligned run of 4 rows one row, drawn from the seed, is the single document 0, 1, ..., 1023.
All inputs are finite; a program needn't handle non-finite values.
Results may differ from the reference program's by a relative error of at most 0.024.
Values may be sent and summed in bfloat16 or wider, within the bound.
A program may use at most 320 MiB of HBM per device.

```python
import math
import jax
import jax.numpy as jnp
from jax import lax

D = 960
FF = 2560
HQ = 15
KVH = 5
HD = 64
SEQS = 4
LENGTH = 1024
SEQUENCES = 64


def draw_positions(key, part):
    key = jax.random.fold_in(key, 11)
    split_keys = jax.random.split(key, 2)
    place_index = jnp.arange(LENGTH, dtype=jnp.int32)
    random_rolls = jax.random.randint(split_keys[0], (SEQUENCES, LENGTH), 0, LENGTH)
    chosen = jax.random.randint(split_keys[1], (SEQUENCES // SEQS,), 0, SEQS)
    member = jnp.arange(SEQUENCES, dtype=jnp.int32) % SEQS
    single = member == jnp.repeat(chosen, SEQS)
    starts = (random_rolls < 3) | (place_index[None, :] == 0)
    starts = jnp.where(single[:, None], place_index[None, :] == 0, starts)
    latest = lax.cummax(jnp.where(starts, place_index[None, :], 0), axis=1)
    return (place_index[None, :] - latest).astype(jnp.int32)


def block_scale(own_key, dims, cuts, least, high):
    level, own = 1.0, jax.random.fold_in(own_key, 6)
    for dim, shards_of in cuts:
        steps = jnp.exp(jax.random.uniform(jax.random.fold_in(own, dim), (shards_of,), jnp.float32, least / len(cuts), high / len(cuts)))
        level = level * jnp.repeat(steps, dims[dim] // shards_of).reshape([-1 if axis == dim else 1 for axis in range(len(dims))])
    return level


def bell_draw(stream_key, extent, deviation, limit, cuts=(), kind=jnp.bfloat16):
    values = jax.random.normal(stream_key, extent, jnp.float32) * deviation
    if len(cuts) > 0:
        values = block_scale(stream_key, extent, cuts, -0.22, 0.18) * values
    return jnp.clip(values, min=-limit, max=limit).astype(kind)


def setup_inputs(seed: int = 0) -> dict:
    keys = jax.random.split(jax.random.key(seed), 13)
    tokens = bell_draw(keys[0], (SEQUENCES, LENGTH, D), 1.0, 6.0, ((0, 16), (1, 2)))
    positions = draw_positions(jax.random.fold_in(keys[12], 71), 0)
    attn_gain = jnp.clip(1.0 + 0.15 * jax.random.normal(keys[2], (D,), jnp.float32), 0.25, 1.75).astype(jnp.bfloat16)
    w_query = bell_draw(keys[3], (D, HQ * HD), (D // 4) ** -0.5, 0.375, ((0, 2),))
    w_key = bell_draw(keys[4], (D, KVH * HD), D ** -0.5, 0.1875, ((0, 2),))
    w_value = bell_draw(keys[5], (D, KVH * HD), D ** -0.5, 0.1875, ((0, 2),))
    w_out = bell_draw(keys[6], (HQ * HD, D), (HQ * HD // 8) ** -0.5, 0.5, ((0, 2),))
    mlp_gain = jnp.clip(1.0 + 0.15 * jax.random.normal(keys[7], (D,), jnp.float32), 0.25, 1.75).astype(jnp.bfloat16)
    w_gate = bell_draw(keys[8], (D, FF), D ** -0.5, 0.1875, ((0, 2),))
    w_up = bell_draw(keys[9], (D, FF), D ** -0.5, 0.1875, ((0, 2),))
    w_down = bell_draw(keys[10], (FF, D), FF ** -0.5, 0.125, ((0, 2),))
    cotangent = bell_draw(keys[11], (SEQUENCES, LENGTH, D), 1.0, 6.0, ((0, 16), (1, 2)))
    return {"tokens": tokens, "positions": positions, "attn_gain": attn_gain, "w_query": w_query, "w_key": w_key, "w_value": w_value, "w_out": w_out, "mlp_gain": mlp_gain, "w_gate": w_gate, "w_up": w_up, "w_down": w_down, "cotangent": cotangent}


NORM_EPSILON = 1e-05
ROPE_BASE = 100000.0
HIGHEST = lax.Precision.HIGHEST

@jax.custom_vjp
def low(v):
    return lax.optimization_barrier(v.astype(jnp.bfloat16)).astype(jnp.float32)

@jax.custom_vjp
def low_back(v):
    return v

def low_keep(v):
    return (low(v), None)

def low_pass(kept, grad):
    return (grad,)

def back_keep(v):
    return (v, None)

def back_low(kept, grad):
    return (low(grad),)
low.defvjp(low_keep, low_pass)
low_back.defvjp(back_keep, back_low)

def normalize(values, gain_row):
    return values * lax.rsqrt(lax.optimization_barrier(jnp.mean(values * values, -1, keepdims=True)) + NORM_EPSILON) * gain_row

def rotate(values, places, head_count):
    shaped = values.reshape(values.shape[0], values.shape[1], head_count, -1)
    half_size = shaped.shape[-1] // 2
    frequency = ROPE_BASE ** (-jnp.arange(half_size, dtype=jnp.float32) * 2.0 / (2 * half_size))
    angles = places.astype(jnp.float32)[:, :, None] * frequency[None, None, :]
    cosine = jnp.cos(angles)[:, :, None, :]
    sine_part = jnp.sin(angles)[:, :, None, :]
    first_half = shaped[..., :half_size]
    second_half = shaped[..., half_size:]
    turned = jnp.concatenate([first_half * cosine - second_half * sine_part, second_half * cosine + first_half * sine_part], -1)
    return turned.reshape(values.shape)

def project(left_side, weight):
    return jnp.einsum('bld,de->ble', left_side, weight, precision=HIGHEST)

def attend(query_rows, key_rows, value_rows, places):
    batch_rows = query_rows.shape[0]
    length = query_rows.shape[1]
    group_width = HQ // KVH
    block_rows = min(512, length)
    block_count = length // block_rows
    query_blocks = jnp.transpose(query_rows.reshape(batch_rows, block_count, block_rows, KVH, group_width, HD), (1, 0, 2, 3, 4, 5))
    place_blocks = jnp.transpose(places.reshape(batch_rows, block_count, block_rows), (1, 0, 2))
    keys_split = key_rows.reshape(batch_rows, length, KVH, HD)
    values_split = value_rows.reshape(batch_rows, length, KVH, HD)
    key_index = jnp.arange(length, dtype=jnp.int32)
    scale_factor = HD ** (-0.5)

    def one_block(block_parts):
        query_block, place_block, block_start = block_parts
        scores = low_back(jnp.einsum('bqhgd,bkhd->bhgqk', query_block, keys_split, precision=HIGHEST) * scale_factor)
        query_index = block_start + jnp.arange(block_rows, dtype=jnp.int32)
        doc_start = query_index[None, :] - place_block
        allowed = (key_index[None, None, :] <= query_index[None, :, None]) & (key_index[None, None, :] >= doc_start[:, :, None])
        masked = jnp.where(allowed[:, None, None], scores, -1e+30)
        weights = jnp.exp(masked - lax.optimization_barrier(jnp.max(masked, -1, keepdims=True)))
        prob_rows = low(weights / lax.optimization_barrier(jnp.sum(weights, -1, keepdims=True)))
        return jnp.einsum('bhgqk,bkhd->bqhgd', prob_rows, values_split, precision=HIGHEST)
    block_starts = jnp.arange(block_count, dtype=jnp.int32) * block_rows
    results = lax.map(jax.checkpoint(one_block), (query_blocks, place_blocks, block_starts))
    return jnp.transpose(results, (1, 0, 2, 3, 4, 5)).reshape(batch_rows, length, HQ * HD)

def block_forward(tokens, w_query, w_key, w_value, w_out, attn_gain, w_gate, w_up, w_down, mlp_gain, places):
    normed_one = low(normalize(tokens, attn_gain))
    query_rows = low(rotate(low_back(project(normed_one, w_query)), places, HQ))
    key_rows = low(rotate(low_back(project(normed_one, w_key)), places, KVH))
    value_rows = low(low_back(project(normed_one, w_value)))
    head_rows = low(low_back(attend(query_rows, key_rows, value_rows, places)))
    mixed_rows = tokens + low_back(project(head_rows, w_out))
    normed_two = low(normalize(mixed_rows, mlp_gain))
    gate_rows = low_back(project(normed_two, w_gate))
    up_rows = low_back(project(normed_two, w_up))
    hidden = low(jax.nn.silu(gate_rows) * up_rows)
    return mixed_rows + low_back(project(hidden, w_down))

def reference(tokens, positions, attn_gain, w_query, w_key, w_value, w_out, mlp_gain, w_gate, w_up, w_down, cotangent):
    sequence_count = tokens.shape[0]
    length = tokens.shape[1]
    batch_rows = math.gcd(sequence_count, max(1, 4096 // length))
    step_count = sequence_count // batch_rows
    params = tuple((weight.astype(jnp.float32) for weight in (w_query, w_key, w_value, w_out, attn_gain, w_gate, w_up, w_down, mlp_gain)))
    token_steps = tokens.reshape(step_count, batch_rows, length, D)
    place_steps = positions.reshape(step_count, batch_rows, length)
    grad_steps = cotangent.reshape(step_count, batch_rows, length, D)

    def one_step(grad_sums, step_parts):
        token_block, place_block, grad_block = step_parts

        def apply_layer(inputs, *weights):
            return block_forward(inputs, *weights, place_block)
        result, pull_back = jax.vjp(apply_layer, token_block.astype(jnp.float32), *params)
        gradients = pull_back(grad_block.astype(jnp.float32))
        new_sums = tuple((running + addend for running, addend in zip(grad_sums, gradients[1:])))
        return (new_sums, (result.astype(jnp.bfloat16), gradients[0]))
    start_sums = tuple((jnp.zeros_like(weight) for weight in params))
    grad_sums, (outputs, input_grads) = lax.scan(one_step, start_sums, (token_steps, place_steps, grad_steps))
    return (outputs.reshape(sequence_count, length, D), input_grads.reshape(sequence_count, length, D), grad_sums[4], grad_sums[0], grad_sums[1], grad_sums[2], grad_sums[3], grad_sums[8], grad_sums[5], grad_sums[6], grad_sums[7])
```

```python
import functools

import jax
import jax.numpy as jnp
from jax import lax
from jax.experimental import pallas as pl
from jax.experimental.pallas import tpu as pltpu
from jax.sharding import PartitionSpec as P

HQ = 15
KVH = 5
HD = 64
GROUP = HQ // KVH
BLOCK = 256


NORM_EPSILON = 1e-05
ROPE_BASE = 100000.0


def normalize(values, gain_row):
    return (
        values * lax.rsqrt(jnp.mean(values * values, -1, keepdims=True) + NORM_EPSILON) * gain_row
    )


def turn(values, cosine, sine_part):
    half = HD // 2
    first_half = values[..., :half, :]
    second_half = values[..., half:, :]
    return jnp.concatenate(
        [
            first_half * cosine - second_half * sine_part,
            second_half * cosine + first_half * sine_part,
        ],
        -2,
    )


def rotate_heads(values, cosine, sine_part):
    shaped = values.reshape(values.shape[0], -1, HD, values.shape[2])
    return turn(shaped, cosine[:, None], sine_part[:, None]).reshape(values.shape)


def mm(a, b):
    return lax.dot_general(a, b, (((1,), (0,)), ((), ())), preferred_element_type=jnp.float32)


def tile_rows(rows):
    return min(BLOCK, rows)


def tile_bias(tile, query_first, start_row):
    size = start_row.shape[1]
    keys = tile * size + lax.broadcasted_iota(jnp.int32, (size, size), 0)
    queries = query_first + lax.broadcasted_iota(jnp.int32, (size, size), 1)
    return jnp.where((keys <= queries) & (keys >= start_row), 0.0, -1e30)


def attend_kernel(
    meta, query_ref, cos_ref, sin_ref, key_ref, value_ref, start_ref,
    out_ref, turned_ref, log_ref, keys_flat,
):
    seq = pl.program_id(0)
    pieces, rows = key_ref.shape[0], key_ref.shape[3]
    tile_size = tile_rows(rows)
    per_piece = rows // tile_size
    for piece in range(pieces):
        keys_flat[piece * rows : (piece + 1) * rows, :] = key_ref[piece, 0].T
    cosine, sine_part = cos_ref[0], sin_ref[0]
    for head in range(GROUP):
        raw = query_ref[0, head * HD : (head + 1) * HD, :]
        turned = turn(raw, cosine, sine_part).astype(jnp.bfloat16)
        turned_ref[0, head * HD : (head + 1) * HD, :] = turned * jnp.bfloat16(HD**-0.5)
    for block in range(per_piece):
        span = slice(block * tile_size, (block + 1) * tile_size)
        low_tile = meta[1 + seq * per_piece + block]
        high_tile = meta[0] * per_piece + block + 1
        query_first = (meta[0] * per_piece + block) * tile_size
        start_row = start_ref[0, :, span]

        def step(tile, carry):
            keys = keys_flat[pl.ds(pl.multiple_of(tile * tile_size, tile_size), tile_size), :]
            offset = pl.multiple_of((tile % per_piece) * tile_size, tile_size)
            values = value_ref[tile // per_piece, 0, :, pl.ds(offset, tile_size)]
            bias = tile_bias(tile, query_first, start_row)
            result = []
            for head in range(GROUP):
                run_max, run_total, run_acc = carry[head]
                scores = mm(keys, turned_ref[0, head * HD : (head + 1) * HD, span]) + bias
                new_max = jnp.maximum(run_max, jnp.max(scores, 0, keepdims=True))
                weights = jnp.exp(scores - new_max)
                factor = jnp.exp(run_max - new_max)
                new_total = run_total * factor + jnp.sum(weights, 0, keepdims=True)
                new_acc = run_acc * factor + mm(values, weights.astype(jnp.bfloat16))
                result.append((new_max, new_total, new_acc))
            return tuple(result)

        start = tuple(
            (
                jnp.full((1, tile_size), -1e30, jnp.float32),
                jnp.zeros((1, tile_size), jnp.float32),
                jnp.zeros((HD, tile_size), jnp.float32),
            )
            for _ in range(GROUP)
        )
        final = lax.fori_loop(low_tile, high_tile, step, start)
        for head in range(GROUP):
            run_max, run_total, run_acc = final[head]
            out_ref[0, head * HD : (head + 1) * HD, span] = (run_acc / run_total).astype(
                jnp.bfloat16
            )
            log_ref[0, 0, head : head + 1, span] = run_max + jnp.log(run_total)


def pull_kernel(
    meta, turned_ref, grad_ref, out_ref, log_ref, cos_ref, sin_ref, key_ref, value_ref, start_ref,
    query_back_ref, key_grad_ref, value_grad_ref,
    keys_flat, values_flat, key_sum, value_sum,
):
    seq = pl.program_id(0)
    pieces, rows = key_ref.shape[0], key_ref.shape[3]
    tile_size = tile_rows(rows)
    per_piece = rows // tile_size
    for piece in range(pieces):
        keys_flat[piece * rows : (piece + 1) * rows, :] = key_ref[piece, 0].T
        values_flat[piece * rows : (piece + 1) * rows, :] = value_ref[piece, 0].T
    key_sum[...] = jnp.zeros_like(key_sum)
    value_sum[...] = jnp.zeros_like(value_sum)
    for block in range(per_piece):
        span = slice(block * tile_size, (block + 1) * tile_size)
        low_tile = meta[1 + seq * per_piece + block]
        high_tile = meta[0] * per_piece + block + 1
        query_first = (meta[0] * per_piece + block) * tile_size
        start_row = start_ref[0, :, span]
        query_side, deltas = [], []
        for head in range(GROUP):
            query_cols = turned_ref[0, head * HD : (head + 1) * HD, span]
            grad_cols = grad_ref[0, head * HD : (head + 1) * HD, span]
            out_cols = out_ref[0, head * HD : (head + 1) * HD, span]
            deltas.append(
                jnp.sum(
                    grad_cols.astype(jnp.float32) * out_cols.astype(jnp.float32), 0, keepdims=True
                )
            )
            query_side.append((query_cols.T, grad_cols.T))

        def step(tile, carry):
            where = pl.ds(pl.multiple_of(tile * tile_size, tile_size), tile_size)
            keys = keys_flat[where, :]
            values = values_flat[where, :]
            offset = pl.multiple_of((tile % per_piece) * tile_size, tile_size)
            keys_across = key_ref[tile // per_piece, 0, :, pl.ds(offset, tile_size)]
            bias = tile_bias(tile, query_first, start_row)
            key_part = key_sum[where, :]
            value_part = value_sum[where, :]
            result = []
            for head in range(GROUP):
                rows_of = slice(head * HD, (head + 1) * HD)
                scores = mm(keys, turned_ref[0, rows_of, span]) + bias
                probs = jnp.exp(scores - log_ref[0, 0, head : head + 1, span])
                prob_grad = mm(values, grad_ref[0, rows_of, span])
                score_grad = (probs * (prob_grad - deltas[head])).astype(jnp.bfloat16)
                result.append(carry[head] + mm(keys_across, score_grad))
                key_part += mm(score_grad, query_side[head][0])
                value_part += mm(probs.astype(jnp.bfloat16), query_side[head][1])
            key_sum[where, :] = key_part
            value_sum[where, :] = value_part
            return tuple(result)

        final = lax.fori_loop(
            low_tile,
            high_tile,
            step,
            tuple(jnp.zeros((HD, tile_size), jnp.float32) for _ in range(GROUP)),
        )
        for head in range(GROUP):
            query_back_ref[0, head * HD : (head + 1) * HD, span] = turn(
                final[head] * (HD**-0.5), cos_ref[0, :, span], -sin_ref[0, :, span]
            ).astype(jnp.bfloat16)
    for piece in range(pieces):
        where = slice(piece * rows, (piece + 1) * rows)
        key_grad_ref[piece, 0] = key_sum[where, :].T.astype(jnp.bfloat16)
        value_grad_ref[piece, 0] = value_sum[where, :].T.astype(jnp.bfloat16)


def head_specs(pieces, rows):
    return dict(
        heads=pl.BlockSpec((1, GROUP * HD, rows), lambda s, g, m: (s, g, 0)),
        angle=pl.BlockSpec((1, HD // 2, rows), lambda s, g, m: (s, 0, 0)),
        key=pl.BlockSpec((pieces, 1, HD, rows), lambda s, g, m: (0, s, g, 0)),
        value=pl.BlockSpec((pieces, 1, HD, rows), lambda s, g, m: (0, s, KVH + g, 0)),
        start=pl.BlockSpec((1, 1, rows), lambda s, g, m: (s, 0, 0)),
        log=pl.BlockSpec((1, 1, GROUP, rows), lambda s, g, m: (s, g, 0, 0)),
    )


def attend(meta, query_raw, cosine, sine_part, pairs, doc_start):
    pieces, seqs, _, rows = pairs.shape
    spec = head_specs(pieces, rows)
    work = seqs * HQ * rows * rows * pieces * HD
    return pl.pallas_call(
        attend_kernel,
        grid_spec=pltpu.PrefetchScalarGridSpec(
            num_scalar_prefetch=1,
            grid=(seqs, KVH),
            in_specs=[
                spec["heads"], spec["angle"], spec["angle"], spec["key"], spec["value"],
                spec["start"],
            ],
            out_specs=[spec["heads"], spec["heads"], spec["log"]],
            scratch_shapes=[pltpu.VMEM((pieces * rows, HD), jnp.bfloat16)],
        ),
        out_shape=[
            jax.ShapeDtypeStruct((seqs, HQ * HD, rows), jnp.bfloat16),
            jax.ShapeDtypeStruct((seqs, HQ * HD, rows), jnp.bfloat16),
            jax.ShapeDtypeStruct((seqs, KVH, GROUP, rows), jnp.float32),
        ],
        compiler_params=pltpu.CompilerParams(vmem_limit_bytes=32 * 1024 * 1024),
        cost_estimate=pl.CostEstimate(
            flops=16 * work, bytes_accessed=32 * 1024 * 1024, transcendentals=work // HD
        ),
        name="attend",
    )(meta, query_raw, cosine, sine_part, pairs, pairs, doc_start)


def attend_pull(meta, turned, heads_grad, heads_out, log_total, cosine, sine_part, pairs, doc_start):
    pieces, seqs, _, rows = pairs.shape
    spec = head_specs(pieces, rows)
    work = seqs * HQ * rows * rows * pieces * HD
    return pl.pallas_call(
        pull_kernel,
        grid_spec=pltpu.PrefetchScalarGridSpec(
            num_scalar_prefetch=1,
            grid=(seqs, KVH),
            in_specs=[
                spec["heads"], spec["heads"], spec["heads"], spec["log"], spec["angle"],
                spec["angle"], spec["key"], spec["value"], spec["start"],
            ],
            out_specs=[spec["heads"], spec["key"], spec["key"]],
            scratch_shapes=[
                pltpu.VMEM((pieces * rows, HD), jnp.bfloat16),
                pltpu.VMEM((pieces * rows, HD), jnp.bfloat16),
                pltpu.VMEM((pieces * rows, HD), jnp.float32),
                pltpu.VMEM((pieces * rows, HD), jnp.float32),
            ],
        ),
        out_shape=[
            jax.ShapeDtypeStruct((seqs, HQ * HD, rows), jnp.bfloat16),
            jax.ShapeDtypeStruct((pieces, seqs, KVH * HD, rows), jnp.bfloat16),
            jax.ShapeDtypeStruct((pieces, seqs, KVH * HD, rows), jnp.bfloat16),
        ],
        compiler_params=pltpu.CompilerParams(vmem_limit_bytes=32 * 1024 * 1024),
        cost_estimate=pl.CostEstimate(
            flops=40 * work, bytes_accessed=48 * 1024 * 1024, transcendentals=work // HD
        ),
        name="attend_pull",
    )(meta, turned, heads_grad, heads_out, log_total, cosine, sine_part, pairs, pairs, doc_start)


def project_rows(left_side, weight):
    return jnp.einsum("sqd,de->sqe", left_side, weight, preferred_element_type=jnp.float32)


def project_across(left_side, weight):
    return jnp.einsum("sqd,de->seq", left_side, weight, preferred_element_type=jnp.float32)


def back_across(grad_rows, weight):
    return jnp.einsum("seq,de->sqd", grad_rows, weight, preferred_element_type=jnp.float32)


def weight_grad_across(left_side, grad_rows):
    return jnp.einsum("sqd,seq->de", left_side, grad_rows, preferred_element_type=jnp.float32)


def project_back(grad_rows, weight):
    return jnp.einsum("sqe,de->sqd", grad_rows, weight, preferred_element_type=jnp.float32)


def weight_grad(left_side, grad_rows):
    return jnp.einsum("sqd,sqe->de", left_side, grad_rows, preferred_element_type=jnp.float32)


def gated(gate_in, up_in):
    return jax.nn.silu(gate_in) * up_in


def body(
    tokens,
    positions,
    attn_gain,
    w_query,
    w_key,
    w_value,
    w_out,
    mlp_gain,
    w_gate,
    w_up,
    w_down,
    cotangent,
):
    seq_local = tokens.shape[0]
    rows_local = tokens.shape[1]
    shard = lax.axis_index("shard")
    query_index = shard * rows_local + jnp.arange(rows_local, dtype=jnp.int32)
    doc_start = query_index[None, :] - positions
    tile_size = tile_rows(rows_local)
    meta = jnp.concatenate(
        [
            jnp.reshape(shard, (1,)).astype(jnp.int32),
            jnp.reshape(doc_start[:, ::tile_size] // tile_size, (-1,)),
        ]
    )
    start_rows = doc_start[:, None, :]
    frequency = ROPE_BASE ** (-jnp.arange(HD // 2, dtype=jnp.float32) * 2.0 / HD)
    angles = positions.astype(jnp.float32)[:, None, :] * frequency[None, :, None]
    cosine, sine_part = jnp.cos(angles), jnp.sin(angles)
    full_query, full_key, full_value, full_out, first_gain = (
        lax.all_gather(w_query, "shard", axis=0, tiled=True),
        lax.all_gather(w_key, "shard", axis=0, tiled=True),
        lax.all_gather(w_value, "shard", axis=0, tiled=True),
        lax.all_gather(w_out, "shard", axis=0, tiled=True),
        lax.all_gather(attn_gain, "shard", axis=0, tiled=True),
    )
    tokens_wide = tokens.astype(jnp.float32)
    normed_one = normalize(tokens_wide, first_gain.astype(jnp.float32)).astype(jnp.bfloat16)
    key_rot = rotate_heads(project_across(normed_one, full_key), cosine, sine_part)
    value_rows = project_across(normed_one, full_value)
    pairs = lax.all_gather(
        jnp.concatenate([key_rot.astype(jnp.bfloat16), value_rows.astype(jnp.bfloat16)], 1),
        "shard",
        axis=0,
    )
    query_raw = project_across(normed_one, full_query)
    heads_out, query_rot, log_total = attend(
        meta, query_raw, cosine, sine_part, pairs, start_rows
    )
    mixed_rows = tokens_wide + jnp.einsum(
        "seq,ed->sqd", heads_out, full_out, preferred_element_type=jnp.float32
    )
    full_gate, full_up, full_down, second_gain = (
        lax.all_gather(w_gate, "shard", axis=0, tiled=True),
        lax.all_gather(w_up, "shard", axis=0, tiled=True),
        lax.all_gather(w_down, "shard", axis=0, tiled=True),
        lax.all_gather(mlp_gain, "shard", axis=0, tiled=True),
    )
    normed_two = normalize(mixed_rows, second_gain.astype(jnp.float32)).astype(jnp.bfloat16)
    gate_rows = project_rows(normed_two, full_gate).astype(jnp.bfloat16).astype(jnp.float32)
    up_rows = project_rows(normed_two, full_up).astype(jnp.bfloat16).astype(jnp.float32)
    hidden = gated(gate_rows, up_rows).astype(jnp.bfloat16)
    output = (mixed_rows + project_rows(hidden, full_down)).astype(jnp.bfloat16)
    hidden_grad = project_back(cotangent, full_down)
    gated_again, gated_pull = jax.vjp(gated, gate_rows, up_rows)
    gate_wide, up_wide = gated_pull(hidden_grad)
    gate_grad = gate_wide.astype(jnp.bfloat16)
    up_grad = up_wide.astype(jnp.bfloat16)
    normed_two_grad = project_back(gate_grad, full_gate) + project_back(up_grad, full_up)
    norm_again, norm_pull = jax.vjp(normalize, mixed_rows, second_gain.astype(jnp.float32))
    mixed_part, second_gain_grad = norm_pull(normed_two_grad)
    mixed_grad = cotangent.astype(jnp.float32) + mixed_part
    down_grad = weight_grad(hidden, cotangent)
    gate_weight_grad = weight_grad(normed_two, gate_grad)
    up_weight_grad = weight_grad(normed_two, up_grad)
    mlp_owned = (
        lax.psum_scatter(
            gate_weight_grad.astype(jnp.bfloat16), "shard", scatter_dimension=0, tiled=True
        ),
        lax.psum_scatter(
            up_weight_grad.astype(jnp.bfloat16), "shard", scatter_dimension=0, tiled=True
        ),
        lax.psum_scatter(
            down_grad.astype(jnp.bfloat16), "shard", scatter_dimension=0, tiled=True
        ),
        lax.psum_scatter(
            second_gain_grad.astype(jnp.bfloat16), "shard", scatter_dimension=0, tiled=True
        ),
    )
    mlp_summed = tuple(lax.psum(part, "dp") for part in mlp_owned)
    branch_grad = mixed_grad.astype(jnp.bfloat16)
    out_weight_grad = jnp.einsum(
        "seq,sqd->ed", heads_out, branch_grad, preferred_element_type=jnp.float32
    )
    heads_grad = jnp.einsum(
        "sqd,ed->seq", branch_grad, full_out, preferred_element_type=jnp.float32
    ).astype(jnp.bfloat16)
    query_back, key_grads, value_grads = attend_pull(
        meta, query_rot, heads_grad, heads_out, log_total, cosine, sine_part, pairs, start_rows
    )
    key_share = lax.psum_scatter(key_grads, "shard", scatter_dimension=0, tiled=False)
    value_back = lax.psum_scatter(value_grads, "shard", scatter_dimension=0, tiled=False)
    key_back = rotate_heads(key_share.astype(jnp.float32), cosine, -sine_part).astype(jnp.bfloat16)
    query_weight_grad = weight_grad_across(normed_one, query_back)
    key_weight_grad = weight_grad_across(normed_one, key_back)
    value_weight_grad = weight_grad_across(normed_one, value_back)
    normed_one_grad = (
        back_across(query_back, full_query)
        + back_across(key_back, full_key)
        + back_across(value_back, full_value)
    )
    first_again, first_pull = jax.vjp(normalize, tokens_wide, first_gain.astype(jnp.float32))
    token_part, first_gain_grad = first_pull(normed_one_grad)
    input_grad = mixed_grad + token_part
    attn_owned = (
        lax.psum_scatter(
            query_weight_grad.astype(jnp.bfloat16), "shard", scatter_dimension=0, tiled=True
        ),
        lax.psum_scatter(
            key_weight_grad.astype(jnp.bfloat16), "shard", scatter_dimension=0, tiled=True
        ),
        lax.psum_scatter(
            value_weight_grad.astype(jnp.bfloat16), "shard", scatter_dimension=0, tiled=True
        ),
        lax.psum_scatter(
            out_weight_grad.astype(jnp.bfloat16), "shard", scatter_dimension=0, tiled=True
        ),
        lax.psum_scatter(
            first_gain_grad.astype(jnp.bfloat16), "shard", scatter_dimension=0, tiled=True
        ),
    )
    attn_owned, mlp_summed = lax.optimization_barrier((attn_owned, mlp_summed))
    summed = tuple(lax.psum(part, "dp").astype(jnp.float32) for part in attn_owned) + tuple(
        part.astype(jnp.float32) for part in mlp_summed
    )
    return (
        output,
        input_grad,
        summed[4],
        summed[0],
        summed[1],
        summed[2],
        summed[3],
        summed[8],
        summed[5],
        summed[6],
        summed[7],
    )


def solution(mesh):
    in_specs = (
        P("dp", "shard", None),
        P("dp", "shard"),
        P("shard"),
        P("shard", None),
        P("shard", None),
        P("shard", None),
        P("shard", None),
        P("shard"),
        P("shard", None),
        P("shard", None),
        P("shard", None),
        P("dp", "shard", None),
    )
    out_specs = (
        P("dp", "shard", None),
        P("dp", "shard", None),
        P("shard"),
        P("shard", None),
        P("shard", None),
        P("shard", None),
        P("shard", None),
        P("shard"),
        P("shard", None),
        P("shard", None),
        P("shard", None),
    )
    return jax.shard_map(body, mesh=mesh, in_specs=in_specs, out_specs=out_specs, check_vma=False)
```

```python
import jax
import jax.numpy as jnp
from jax import lax
from jax.experimental import pallas as pl
from jax.experimental.pallas import tpu as pltpu
from jax.sharding import PartitionSpec as P

HQ = 15
KVH = 5
HD = 64
GROUP = HQ // KVH
BLOCK = 256


NORM_EPSILON = 1e-05
ROPE_BASE = 100000.0


def normalize(values, gain_row):
    return (
        values * lax.rsqrt(jnp.mean(values * values, -1, keepdims=True) + NORM_EPSILON) * gain_row
    )


def turn(values, cosine, sine_part):
    half = HD // 2
    first_half = values[..., :half, :]
    second_half = values[..., half:, :]
    return jnp.concatenate(
        [
            first_half * cosine - second_half * sine_part,
            second_half * cosine + first_half * sine_part,
        ],
        -2,
    )


def rotate_heads(values, cosine, sine_part):
    shaped = values.reshape(values.shape[0], -1, HD, values.shape[2])
    return turn(shaped, cosine[:, None], sine_part[:, None]).reshape(values.shape)


def mm(a, b):
    return lax.dot_general(a, b, (((1,), (0,)), ((), ())), preferred_element_type=jnp.float32)


def tile_rows(rows):
    return min(BLOCK, rows)


def tile_bias(tile, query_first, start_row):
    size = start_row.shape[1]
    keys = tile * size + lax.broadcasted_iota(jnp.int32, (size, size), 0)
    queries = query_first + lax.broadcasted_iota(jnp.int32, (size, size), 1)
    return jnp.where((keys <= queries) & (keys >= start_row), 0.0, -1e30)


def attend_kernel(
    meta, query_ref, cos_ref, sin_ref, key_ref, value_ref, start_ref,
    out_ref, turned_ref, log_ref, keys_flat,
):
    seq = pl.program_id(0)
    pieces, rows = key_ref.shape[0], key_ref.shape[3]
    tile_size = tile_rows(rows)
    per_piece = rows // tile_size
    for piece in range(pieces):
        keys_flat[piece * rows : (piece + 1) * rows, :] = key_ref[piece, 0].T
    cosine, sine_part = cos_ref[0], sin_ref[0]
    for head in range(GROUP):
        raw = query_ref[0, head * HD : (head + 1) * HD, :]
        turned = turn(raw, cosine, sine_part).astype(jnp.bfloat16)
        turned_ref[0, head * HD : (head + 1) * HD, :] = turned * jnp.bfloat16(HD**-0.5)
    for block in range(per_piece):
        span = slice(block * tile_size, (block + 1) * tile_size)
        low_tile = meta[1 + seq * per_piece + block]
        high_tile = meta[0] * per_piece + block + 1
        query_first = (meta[0] * per_piece + block) * tile_size
        start_row = start_ref[0, :, span]

        def step(tile, carry):
            keys = keys_flat[pl.ds(pl.multiple_of(tile * tile_size, tile_size), tile_size), :]
            offset = pl.multiple_of((tile % per_piece) * tile_size, tile_size)
            values = value_ref[tile // per_piece, 0, :, pl.ds(offset, tile_size)]
            bias = tile_bias(tile, query_first, start_row)
            result = []
            for head in range(GROUP):
                run_max, run_total, run_acc = carry[head]
                scores = mm(keys, turned_ref[0, head * HD : (head + 1) * HD, span]) + bias
                new_max = jnp.maximum(run_max, jnp.max(scores, 0, keepdims=True))
                weights = jnp.exp(scores - new_max)
                factor = jnp.exp(run_max - new_max)
                new_total = run_total * factor + jnp.sum(weights, 0, keepdims=True)
                new_acc = run_acc * factor + mm(values, weights.astype(jnp.bfloat16))
                result.append((new_max, new_total, new_acc))
            return tuple(result)

        start = tuple(
            (
                jnp.full((1, tile_size), -1e30, jnp.float32),
                jnp.zeros((1, tile_size), jnp.float32),
                jnp.zeros((HD, tile_size), jnp.float32),
            )
            for _ in range(GROUP)
        )
        final = lax.fori_loop(low_tile, high_tile, step, start)
        for head in range(GROUP):
            run_max, run_total, run_acc = final[head]
            out_ref[0, head * HD : (head + 1) * HD, span] = (run_acc / run_total).astype(
                jnp.bfloat16
            )
            log_ref[0, 0, head : head + 1, span] = run_max + jnp.log(run_total)


def pull_kernel(
    meta, turned_ref, grad_ref, out_ref, log_ref, cos_ref, sin_ref, key_ref, value_ref, start_ref,
    query_back_ref, key_grad_ref, value_grad_ref,
    keys_flat, values_flat, key_sum, value_sum,
):
    seq = pl.program_id(0)
    pieces, rows = key_ref.shape[0], key_ref.shape[3]
    tile_size = tile_rows(rows)
    per_piece = rows // tile_size
    for piece in range(pieces):
        keys_flat[piece * rows : (piece + 1) * rows, :] = key_ref[piece, 0].T
        values_flat[piece * rows : (piece + 1) * rows, :] = value_ref[piece, 0].T
    key_sum[...] = jnp.zeros_like(key_sum)
    value_sum[...] = jnp.zeros_like(value_sum)
    for block in range(per_piece):
        span = slice(block * tile_size, (block + 1) * tile_size)
        low_tile = meta[1 + seq * per_piece + block]
        high_tile = meta[0] * per_piece + block + 1
        query_first = (meta[0] * per_piece + block) * tile_size
        start_row = start_ref[0, :, span]
        query_side, deltas = [], []
        for head in range(GROUP):
            query_cols = turned_ref[0, head * HD : (head + 1) * HD, span]
            grad_cols = grad_ref[0, head * HD : (head + 1) * HD, span]
            out_cols = out_ref[0, head * HD : (head + 1) * HD, span]
            deltas.append(
                jnp.sum(
                    grad_cols.astype(jnp.float32) * out_cols.astype(jnp.float32), 0, keepdims=True
                )
            )
            query_side.append((query_cols.T, grad_cols.T))

        def step(tile, carry):
            where = pl.ds(pl.multiple_of(tile * tile_size, tile_size), tile_size)
            keys = keys_flat[where, :]
            values = values_flat[where, :]
            offset = pl.multiple_of((tile % per_piece) * tile_size, tile_size)
            keys_across = key_ref[tile // per_piece, 0, :, pl.ds(offset, tile_size)]
            bias = tile_bias(tile, query_first, start_row)
            key_part = key_sum[where, :]
            value_part = value_sum[where, :]
            result = []
            for head in range(GROUP):
                rows_of = slice(head * HD, (head + 1) * HD)
                scores = mm(keys, turned_ref[0, rows_of, span]) + bias
                probs = jnp.exp(scores - log_ref[0, 0, head : head + 1, span])
                prob_grad = mm(values, grad_ref[0, rows_of, span])
                score_grad = (probs * (prob_grad - deltas[head])).astype(jnp.bfloat16)
                result.append(carry[head] + mm(keys_across, score_grad))
                key_part += mm(score_grad, query_side[head][0])
                value_part += mm(probs.astype(jnp.bfloat16), query_side[head][1])
            key_sum[where, :] = key_part
            value_sum[where, :] = value_part
            return tuple(result)

        final = lax.fori_loop(
            low_tile,
            high_tile,
            step,
            tuple(jnp.zeros((HD, tile_size), jnp.float32) for _ in range(GROUP)),
        )
        for head in range(GROUP):
            query_back_ref[0, head * HD : (head + 1) * HD, span] = turn(
                final[head] * (HD**-0.5), cos_ref[0, :, span], -sin_ref[0, :, span]
            ).astype(jnp.bfloat16)
    for piece in range(pieces):
        where = slice(piece * rows, (piece + 1) * rows)
        key_grad_ref[piece, 0] = key_sum[where, :].T.astype(jnp.bfloat16)
        value_grad_ref[piece, 0] = value_sum[where, :].T.astype(jnp.bfloat16)


def head_specs(pieces, rows):
    return dict(
        heads=pl.BlockSpec((1, GROUP * HD, rows), lambda s, g, m: (s, g, 0)),
        angle=pl.BlockSpec((1, HD // 2, rows), lambda s, g, m: (s, 0, 0)),
        key=pl.BlockSpec((pieces, 1, HD, rows), lambda s, g, m: (0, s, g, 0)),
        value=pl.BlockSpec((pieces, 1, HD, rows), lambda s, g, m: (0, s, KVH + g, 0)),
        start=pl.BlockSpec((1, 1, rows), lambda s, g, m: (s, 0, 0)),
        log=pl.BlockSpec((1, 1, GROUP, rows), lambda s, g, m: (s, g, 0, 0)),
    )


def attend(meta, query_raw, cosine, sine_part, pairs, doc_start):
    pieces, seqs, _, rows = pairs.shape
    spec = head_specs(pieces, rows)
    work = seqs * HQ * rows * rows * pieces * HD
    return pl.pallas_call(
        attend_kernel,
        grid_spec=pltpu.PrefetchScalarGridSpec(
            num_scalar_prefetch=1,
            grid=(seqs, KVH),
            in_specs=[
                spec["heads"], spec["angle"], spec["angle"], spec["key"], spec["value"],
                spec["start"],
            ],
            out_specs=[spec["heads"], spec["heads"], spec["log"]],
            scratch_shapes=[pltpu.VMEM((pieces * rows, HD), jnp.bfloat16)],
        ),
        out_shape=[
            jax.ShapeDtypeStruct((seqs, HQ * HD, rows), jnp.bfloat16),
            jax.ShapeDtypeStruct((seqs, HQ * HD, rows), jnp.bfloat16),
            jax.ShapeDtypeStruct((seqs, KVH, GROUP, rows), jnp.float32),
        ],
        compiler_params=pltpu.CompilerParams(vmem_limit_bytes=32 * 1024 * 1024),
        cost_estimate=pl.CostEstimate(
            flops=16 * work, bytes_accessed=32 * 1024 * 1024, transcendentals=work // HD
        ),
        name="attend",
    )(meta, query_raw, cosine, sine_part, pairs, pairs, doc_start)


def attend_pull(meta, turned, heads_grad, heads_out, log_total, cosine, sine_part, pairs, doc_start):
    pieces, seqs, _, rows = pairs.shape
    spec = head_specs(pieces, rows)
    work = seqs * HQ * rows * rows * pieces * HD
    return pl.pallas_call(
        pull_kernel,
        grid_spec=pltpu.PrefetchScalarGridSpec(
            num_scalar_prefetch=1,
            grid=(seqs, KVH),
            in_specs=[
                spec["heads"], spec["heads"], spec["heads"], spec["log"], spec["angle"],
                spec["angle"], spec["key"], spec["value"], spec["start"],
            ],
            out_specs=[spec["heads"], spec["key"], spec["key"]],
            scratch_shapes=[
                pltpu.VMEM((pieces * rows, HD), jnp.bfloat16),
                pltpu.VMEM((pieces * rows, HD), jnp.bfloat16),
                pltpu.VMEM((pieces * rows, HD), jnp.float32),
                pltpu.VMEM((pieces * rows, HD), jnp.float32),
            ],
        ),
        out_shape=[
            jax.ShapeDtypeStruct((seqs, HQ * HD, rows), jnp.bfloat16),
            jax.ShapeDtypeStruct((pieces, seqs, KVH * HD, rows), jnp.bfloat16),
            jax.ShapeDtypeStruct((pieces, seqs, KVH * HD, rows), jnp.bfloat16),
        ],
        compiler_params=pltpu.CompilerParams(vmem_limit_bytes=32 * 1024 * 1024),
        cost_estimate=pl.CostEstimate(
            flops=40 * work, bytes_accessed=48 * 1024 * 1024, transcendentals=work // HD
        ),
        name="attend_pull",
    )(meta, turned, heads_grad, heads_out, log_total, cosine, sine_part, pairs, pairs, doc_start)


def project_rows(left_side, weight):
    return jnp.einsum("sqd,de->sqe", left_side, weight, preferred_element_type=jnp.float32)


def project_across(left_side, weight):
    return jnp.einsum("sqd,de->seq", left_side, weight, preferred_element_type=jnp.float32)


def back_across(grad_rows, weight):
    return jnp.einsum("seq,de->sqd", grad_rows, weight, preferred_element_type=jnp.float32)


def weight_grad_across(left_side, grad_rows):
    return jnp.einsum("sqd,seq->de", left_side, grad_rows, preferred_element_type=jnp.float32)


def project_back(grad_rows, weight):
    return jnp.einsum("sqe,de->sqd", grad_rows, weight, preferred_element_type=jnp.float32)


def weight_grad(left_side, grad_rows):
    return jnp.einsum("sqd,sqe->de", left_side, grad_rows, preferred_element_type=jnp.float32)


def scatter_sum(values):
    count = lax.axis_size("shard")
    index = lax.axis_index("shard")
    size = values.shape[0] // count

    def block(which):
        return lax.dynamic_slice_in_dim(values, which * size, size, 0)

    total = block(index).astype(jnp.float32)
    for step in range(1, count):
        order = [(source, (source + step) % count) for source in range(count)]
        arrived = lax.ppermute(block((index + step) % count), "shard", order)
        total += arrived.astype(jnp.float32)
    return total


def gated(gate_in, up_in):
    return jax.nn.silu(gate_in) * up_in


def body(
    tokens,
    positions,
    attn_gain,
    w_query,
    w_key,
    w_value,
    w_out,
    mlp_gain,
    w_gate,
    w_up,
    w_down,
    cotangent,
):
    seq_local = tokens.shape[0]
    rows_local = tokens.shape[1]
    shard = lax.axis_index("shard")
    query_index = shard * rows_local + jnp.arange(rows_local, dtype=jnp.int32)
    doc_start = query_index[None, :] - positions
    tile_size = tile_rows(rows_local)
    meta = jnp.concatenate(
        [
            jnp.reshape(shard, (1,)).astype(jnp.int32),
            jnp.reshape(doc_start[:, ::tile_size] // tile_size, (-1,)),
        ]
    )
    start_rows = doc_start[:, None, :]
    frequency = ROPE_BASE ** (-jnp.arange(HD // 2, dtype=jnp.float32) * 2.0 / HD)
    angles = positions.astype(jnp.float32)[:, None, :] * frequency[None, :, None]
    cosine, sine_part = jnp.cos(angles), jnp.sin(angles)
    small = lax.all_gather(
        jnp.concatenate([w_key, w_value, attn_gain[:, None], mlp_gain[:, None]], 1),
        "shard",
        axis=0,
        tiled=True,
    )
    pair_width = 2 * KVH * HD
    full_pair = small[:, :pair_width]
    first_gain, second_gain = small[:, pair_width], small[:, pair_width + 1]
    full_query = lax.all_gather(w_query, "shard", axis=0, tiled=True)
    full_out = lax.all_gather(w_out, "shard", axis=0, tiled=True)
    tokens_wide = tokens.astype(jnp.float32)
    normed_one = normalize(tokens_wide, first_gain.astype(jnp.float32)).astype(jnp.bfloat16)
    pair_rows = project_across(normed_one, full_pair)
    key_rot = rotate_heads(pair_rows[:, : KVH * HD], cosine, sine_part)
    pairs = lax.all_gather(
        jnp.concatenate([key_rot, pair_rows[:, KVH * HD :]], 1).astype(jnp.bfloat16),
        "shard",
        axis=0,
    )
    query_raw = project_across(normed_one, full_query)
    heads_out, query_rot, log_total = attend(
        meta, query_raw, cosine, sine_part, pairs, start_rows
    )
    mixed_rows = tokens_wide + jnp.einsum(
        "seq,ed->sqd", heads_out, full_out, preferred_element_type=jnp.float32
    )
    full_gate, full_up, full_down = (
        lax.all_gather(w_gate, "shard", axis=0, tiled=True),
        lax.all_gather(w_up, "shard", axis=0, tiled=True),
        lax.all_gather(w_down, "shard", axis=0, tiled=True),
    )
    normed_two = normalize(mixed_rows, second_gain.astype(jnp.float32)).astype(jnp.bfloat16)
    gate_rows = project_rows(normed_two, full_gate).astype(jnp.bfloat16).astype(jnp.float32)
    up_rows = project_rows(normed_two, full_up).astype(jnp.bfloat16).astype(jnp.float32)
    hidden = gated(gate_rows, up_rows).astype(jnp.bfloat16)
    output = (mixed_rows + project_rows(hidden, full_down)).astype(jnp.bfloat16)
    hidden_grad = project_back(cotangent, full_down)
    gated_again, gated_pull = jax.vjp(gated, gate_rows, up_rows)
    gate_wide, up_wide = gated_pull(hidden_grad)
    gate_grad = gate_wide.astype(jnp.bfloat16)
    up_grad = up_wide.astype(jnp.bfloat16)
    normed_two_grad = project_back(gate_grad, full_gate) + project_back(up_grad, full_up)
    norm_again, norm_pull = jax.vjp(normalize, mixed_rows, second_gain.astype(jnp.float32))
    mixed_part, second_gain_grad = norm_pull(normed_two_grad)
    mixed_grad = cotangent.astype(jnp.float32) + mixed_part
    branch_grad = mixed_grad.astype(jnp.bfloat16)
    down_grad = weight_grad(hidden, cotangent).astype(jnp.bfloat16)
    gate_weight_grad = weight_grad(normed_two, gate_grad).astype(jnp.bfloat16)
    up_weight_grad = weight_grad(normed_two, up_grad).astype(jnp.bfloat16)
    down_grad, gate_weight_grad, up_weight_grad, branch_grad = lax.optimization_barrier(
        (down_grad, gate_weight_grad, up_weight_grad, branch_grad)
    )
    mlp_owned = tuple(
        scatter_sum(part).astype(jnp.bfloat16)
        for part in (down_grad, gate_weight_grad, up_weight_grad)
    )
    mlp_summed = tuple(lax.psum(part, "dp") for part in mlp_owned)
    out_weight_grad = jnp.einsum(
        "seq,sqd->ed", heads_out, branch_grad, preferred_element_type=jnp.float32
    )
    heads_grad = jnp.einsum(
        "sqd,ed->seq", branch_grad, full_out, preferred_element_type=jnp.float32
    ).astype(jnp.bfloat16)
    query_back, key_grads, value_grads = attend_pull(
        meta, query_rot, heads_grad, heads_out, log_total, cosine, sine_part, pairs, start_rows
    )
    key_share = scatter_sum(key_grads.reshape(-1, KVH * HD, rows_local))
    value_share = scatter_sum(value_grads.reshape(-1, KVH * HD, rows_local))
    pair_back = jnp.concatenate(
        [rotate_heads(key_share, cosine, -sine_part), value_share], 1
    ).astype(jnp.bfloat16)
    query_weight_grad = weight_grad_across(normed_one, query_back)
    pair_weight_grad = weight_grad_across(normed_one, pair_back)
    normed_one_grad = back_across(query_back, full_query) + back_across(pair_back, full_pair)
    first_again, first_pull = jax.vjp(normalize, tokens_wide, first_gain.astype(jnp.float32))
    token_part, first_gain_grad = first_pull(normed_one_grad)
    input_grad = mixed_grad + token_part
    small_grad = jnp.concatenate(
        [pair_weight_grad, first_gain_grad[:, None], second_gain_grad[:, None]], 1
    )
    attn_owned = tuple(
        scatter_sum(part.astype(jnp.bfloat16)).astype(jnp.bfloat16)
        for part in (out_weight_grad, query_weight_grad, small_grad)
    )
    attn_owned, mlp_summed = lax.optimization_barrier((attn_owned, mlp_summed))
    out_sum, query_sum, small_sum = (
        lax.psum(part, "dp").astype(jnp.float32) for part in attn_owned
    )
    down_sum, gate_sum, up_sum = (part.astype(jnp.float32) for part in mlp_summed)
    return (
        output,
        input_grad,
        small_sum[:, pair_width],
        query_sum,
        small_sum[:, : KVH * HD],
        small_sum[:, KVH * HD : pair_width],
        out_sum,
        small_sum[:, pair_width + 1],
        gate_sum,
        up_sum,
        down_sum,
    )


def solution(mesh):
    in_specs = (
        P("dp", "shard", None),
        P("dp", "shard"),
        P("shard"),
        P("shard", None),
        P("shard", None),
        P("shard", None),
        P("shard", None),
        P("shard"),
        P("shard", None),
        P("shard", None),
        P("shard", None),
        P("dp", "shard", None),
    )
    out_specs = (
        P("dp", "shard", None),
        P("dp", "shard", None),
        P("shard"),
        P("shard", None),
        P("shard", None),
        P("shard", None),
        P("shard", None),
        P("shard"),
        P("shard", None),
        P("shard", None),
        P("shard", None),
    )
    return jax.shard_map(body, mesh=mesh, in_specs=in_specs, out_specs=out_specs, check_vma=False)
```
